32 devices in a mesh: fsdp: 32 (over z, y, x, core).
Axes of the slice: x: 2, y: 2, z: 4, core: 2. Of those that a mesh axis runs over, the one named last changes fastest.
Arguments:
- tokens: bfloat16 [16384, 768], P('fsdp'), may hold values from -6 to 6
- cotangent: bfloat16 [16384, 768], P('fsdp'), may hold values from -6 to 6
- image_ids: int32 [16384], replicated, may hold values from 0 to 83, as said below
- w_qkv: bfloat16 [1, 768, 2304], P(None, 'fsdp'), may hold values from -0.21875 to 0.21875
- w_out: bfloat16 [1, 768, 768], P(None, 'fsdp'), may hold values from -1.25 to 1.25
- w_up: bfloat16 [1, 768, 3072], P(None, 'fsdp'), may hold values from -0.21875 to 0.21875
- w_down: bfloat16 [1, 3072, 768], P(None, 'fsdp'), may hold values from -0.109375 to 0.109375
- gains: bfloat16 [1, 2, 768], P(None, None, 'fsdp'), may hold values from 0.099609375 to 1.8984375
- shifts: bfloat16 [1, 2, 768], P(None, None, 'fsdp'), may hold values from -1.5 to 1.5
- biases: bfloat16 [1, 4, 768], P(None, None, 'fsdp'), may hold values from -1.5 to 1.5
- bias_up: bfloat16 [1, 3072], P(None, 'fsdp'), may hold values from -1.5 to 1.5
Outputs:
- out: bfloat16 [16384, 768], P('fsdp')
- grad_tokens: float32 [16384, 768], P('fsdp')
- grad_qkv: float32 [1, 768, 2304], P(None, 'fsdp')
- grad_out: float32 [1, 768, 768], P(None, 'fsdp')
- grad_up: float32 [1, 768, 3072], P(None, 'fsdp')
- grad_down: float32 [1, 3072, 768], P(None, 'fsdp')
- grad_gains: float32 [1, 2, 768], P(None, None, 'fsdp')
- grad_shifts: float32 [1, 2, 768], P(None, None, 'fsdp')
- grad_biases: float32 [1, 4, 768], P(None, None, 'fsdp')
- grad_bias_up: float32 [1, 3072], P(None, 'fsdp')
The draws below stay inside these ranges and needn't reach their ends.
Inputs may be any that keep to these rules, and one draw needn't show every extreme that they name: image_ids starts at 0, never falls and rises by at most 1 from one token to the next; every image holds 197 consecutive tokens, except possibly the first and the last image of the stream.
All inputs are finite; a program needn't handle non-finite values.
Results may differ from the reference program's by a relative error of at most 0.0095.
Values may be sent and summed in bfloat16 or wider, within the bound.
A program may use at most 256 MiB of HBM per device.

```python
import jax
import jax.numpy as jnp
from jax import lax

HEADS = 12
HEAD_DIM = 64
D = 768
FF = 3072
IMG = 197
LAYERS = 1
QBLK = 512
TOKENS = 16384


def draw_image_ids(key, part):
    key = jax.random.fold_in(key, 11)
    choices_count = IMG - (TOKENS - 1) % IMG
    offset = jax.random.randint(key, (), 0, choices_count, dtype=jnp.int32)
    return ((jnp.arange(TOKENS, dtype=jnp.int32) + offset) // IMG).astype(jnp.int32)


def levels(rng, extent, cuts, low, largest):
    loudness, own = 1.0, jax.random.fold_in(rng, 6)
    for position, shards_of in cuts:
        steps = jnp.exp(jax.random.uniform(jax.random.fold_in(own, position), (shards_of,), jnp.float32, low / len(cuts), largest / len(cuts)))
        loudness = loudness * jnp.repeat(steps, extent[position] // shards_of).reshape([-1 if axis == position else 1 for axis in range(len(extent))])
    return loudness


def bell_draw(rng, dims, width, reach, pieces=(), kind=jnp.bfloat16):
    drawn = width * jax.random.normal(rng, dims, jnp.float32)
    if pieces:
        drawn = drawn * levels(rng, dims, pieces, -0.22, 0.18)
    return jnp.clip(drawn, -reach, reach).astype(kind)


def setup_inputs(seed: int = 0) -> dict:
    seeds = jax.random.split(jax.random.key(seed), 12)
    tokens = bell_draw(seeds[0], (TOKENS, D), 1.0, 6.0, ((0, 32),))
    cotangent = bell_draw(seeds[1], (TOKENS, D), 1.0, 6.0, ((0, 32),))
    image_ids = draw_image_ids(jax.random.fold_in(seeds[11], 71), 0)
    w_qkv = bell_draw(seeds[3], (LAYERS, D, 3 * D), D ** -0.5, 0.21875, ((1, 32),))
    w_out = bell_draw(seeds[4], (LAYERS, D, D), (D // 32) ** -0.5, 1.25, ((1, 32),))
    w_up = bell_draw(seeds[5], (LAYERS, D, FF), D ** -0.5, 0.21875, ((1, 32),))
    w_down = bell_draw(seeds[6], (LAYERS, FF, D), FF ** -0.5, 0.109375, ((1, 32),))
    gains = jnp.clip(1.0 + 0.18 * jax.random.normal(seeds[7], (LAYERS, 2, D), jnp.float32), 0.099609375, 1.8984375).astype(jnp.bfloat16)
    shifts = bell_draw(seeds[8], (LAYERS, 2, D), 0.3, 1.5, ((2, 32),))
    biases = bell_draw(seeds[9], (LAYERS, 4, D), 0.3, 1.5, ((2, 32),))
    bias_up = bell_draw(seeds[10], (LAYERS, FF), 0.3, 1.5, ((1, 32),))
    return dict(tokens=tokens, cotangent=cotangent, image_ids=image_ids, w_qkv=w_qkv, w_out=w_out, w_up=w_up, w_down=w_down, gains=gains, shifts=shifts, biases=biases, bias_up=bias_up)


@jax.custom_vjp
def low(v):
    return lax.optimization_barrier(v.astype(jnp.bfloat16)).astype(jnp.float32)

@jax.custom_vjp
def low_back(v):
    return v

def low_keep(v):
    return (low(v), None)

def low_pass(kept, grad):
    return (grad,)

def back_keep(v):
    return (v, None)

def back_low(kept, grad):
    return (low(grad),)
low.defvjp(low_keep, low_pass)
low_back.defvjp(back_keep, back_low)
highest = lax.Precision.HIGHEST

def normed(values, gain_vec, shift_vec):
    center = values - lax.optimization_barrier(jnp.mean(values, axis=-1, keepdims=True))
    spread = lax.optimization_barrier(jnp.mean(center * center, axis=-1, keepdims=True))
    return center * lax.rsqrt(spread + 1e-06) * gain_vec + shift_vec

@jax.checkpoint
def attend_block(query_part, key_part, value_part, query_ids, key_ids):
    scores = jnp.einsum('qhd,khd->hqk', query_part, key_part, precision=highest) * HEAD_DIM ** (-0.5)
    scores = low_back(scores)
    same_image = query_ids[:, None] == key_ids[None, :]
    scores = jnp.where(same_image[None], scores, -1e+30)
    row_max = lax.optimization_barrier(jnp.max(scores, axis=-1, keepdims=True))
    exponent = jnp.exp(scores - row_max)
    attention = low(exponent / lax.optimization_barrier(jnp.sum(exponent, axis=-1, keepdims=True)))
    return jnp.einsum('hqk,khd->qhd', attention, value_part, precision=highest)

def attend(query_rows, key_ext, value_ext, ids_ext):
    rim_rows = IMG - 1
    key_span = QBLK + 2 * rim_rows

    def one_block(number):
        offset = number * QBLK
        return attend_block(lax.dynamic_slice_in_dim(query_rows, offset, QBLK, 0), lax.dynamic_slice_in_dim(key_ext, offset, key_span, 0), lax.dynamic_slice_in_dim(value_ext, offset, key_span, 0), lax.dynamic_slice_in_dim(ids_ext, offset + rim_rows, QBLK, 0), lax.dynamic_slice_in_dim(ids_ext, offset, key_span, 0))
    numbers = jnp.arange(query_rows.shape[0] // QBLK, dtype=jnp.int32)
    outputs = lax.map(one_block, numbers)
    return outputs.reshape(query_rows.shape[0], HEADS * HEAD_DIM)

@jax.checkpoint
def feed_block(middle, gain_vec, shift_vec, w_up, bias_up, w_down, bias_down):
    normal_two = low(normed(middle, gain_vec, shift_vec))
    before = low_back(jnp.dot(normal_two, w_up, precision=highest) + bias_up)
    activated = low(jax.nn.gelu(before, approximate=False))
    return middle + low_back(jnp.dot(activated, w_down, precision=highest) + bias_down)

def layer_forward(hidden, params, ids_ext):
    w_qkv, w_out, w_up, w_down, gains, shifts, biases, bias_up = params
    model_width = hidden.shape[1]
    rim_rows = IMG - 1
    normal_one = low(normed(hidden, gains[0], shifts[0]))
    qkv_bias = jnp.concatenate([biases[0], jnp.zeros_like(biases[0]), biases[1]])
    projected = low(low_back(jnp.dot(normal_one, w_qkv, precision=highest) + qkv_bias))
    heads_shape = (hidden.shape[0], HEADS, HEAD_DIM)
    padding = jnp.zeros((rim_rows, HEADS, HEAD_DIM), jnp.float32)
    query_rows = projected[:, :model_width].reshape(heads_shape)
    key_ext = jnp.concatenate([padding, projected[:, model_width:2 * model_width].reshape(heads_shape), padding], axis=0)
    value_ext = jnp.concatenate([padding, projected[:, 2 * model_width:].reshape(heads_shape), padding], axis=0)
    mixed = low(low_back(attend(query_rows, key_ext, value_ext, ids_ext)))
    middle = hidden + low_back(jnp.dot(mixed, w_out, precision=highest) + biases[2])
    blocks = middle.reshape(-1, QBLK, model_width)

    def feed_rows(block):
        return feed_block(block, gains[1], shifts[1], w_up, bias_up, w_down, biases[3])
    return lax.map(feed_rows, blocks).reshape(middle.shape)

def reference(tokens, cotangent, image_ids, w_qkv, w_out, w_up, w_down, gains, shifts, biases, bias_up):
    rim_rows = IMG - 1
    ids_ext = jnp.concatenate([jnp.full((rim_rows,), -1, jnp.int32), image_ids.astype(jnp.int32), jnp.full((rim_rows,), -2, jnp.int32)])
    params = tuple((item.astype(jnp.float32) for item in (w_qkv, w_out, w_up, w_down, gains, shifts, biases, bias_up)))

    def forward(hidden, *weights):
        for level_index in range(LAYERS):
            hidden = layer_forward(hidden, tuple((item[level_index] for item in weights)), ids_ext)
        return hidden
    result, pullback = jax.vjp(forward, tokens.astype(jnp.float32), *params)
    grads = pullback(cotangent.astype(jnp.float32))
    return (result.astype(jnp.bfloat16), grads[0], grads[1], grads[2], grads[3], grads[4], grads[5], grads[6], grads[7], grads[8])
```

```python
import math

import jax
import jax.numpy as jnp
from jax import lax
from jax.experimental import pallas as pl
from jax.experimental.pallas import tpu as pltpu
from jax.sharding import PartitionSpec as P

HEADS = 12
HEAD_DIM = 64
RIM = 208
PAD = 256
QB = 256
LANES = 128
SCALE = HEAD_DIM ** (-0.5)
F32 = jnp.float32
BF16 = jnp.bfloat16


def bit_orders(count):
    bits = int(math.log2(count))
    rest = list(range(1, bits))

    def rotated(by):
        return [0] + rest[by:] + rest[:by]

    return rotated


def partner_pairs(count, bit):
    return [(i, i ^ (1 << bit)) for i in range(count)]


def gather_rows(shard, order):
    count = lax.axis_size("fsdp")
    me = lax.axis_index("fsdp")
    have = []
    block = shard[None]
    for bit in reversed(order):
        other = lax.ppermute(block, "fsdp", partner_pairs(count, bit))
        mine_high = ((me >> bit) & 1) == 1
        low = jnp.where(mine_high, other, block)
        high = jnp.where(mine_high, block, other)
        higher = sum(1 for b in have if b > bit)
        lower = len(have) - higher
        lead = (1 << higher, 1 << lower)
        low = low.reshape(lead + shard.shape)
        high = high.reshape(lead + shard.shape)
        block = jnp.stack([low, high], axis=1).reshape((-1,) + shard.shape)
        have.append(bit)
    return block


def scatter_sum(parts, order, send_type):
    count = lax.axis_size("fsdp")
    me = lax.axis_index("fsdp")
    shape = parts.shape[1:]
    left = set(order)
    block = parts
    for bit in order:
        higher = sum(1 for b in left if b > bit)
        lower = len(left) - 1 - higher
        view = block.reshape((1 << higher, 2, 1 << lower) + shape)
        mine = (me >> bit) & 1
        keep = lax.dynamic_index_in_dim(view, mine, axis=1, keepdims=False)
        give = lax.dynamic_index_in_dim(view, 1 - mine, axis=1, keepdims=False).astype(send_type)
        give = give.reshape((-1,) + shape)
        got = lax.ppermute(give, "fsdp", partner_pairs(count, bit))
        block = keep.reshape((-1,) + shape).astype(F32) + got.astype(F32)
        left.remove(bit)
    return block[0]


def centered(values):
    center = values - jnp.mean(values, axis=-1, keepdims=True)
    scale = lax.rsqrt(jnp.mean(center * center, axis=-1, keepdims=True) + 1e-06)
    return center * scale, scale


def norm_back(grad, normal, scale, gain):
    weighted = grad * gain
    mean_one = jnp.mean(weighted, axis=-1, keepdims=True)
    mean_two = jnp.mean(weighted * normal, axis=-1, keepdims=True)
    return scale * (weighted - mean_one - normal * mean_two)


def outer_sum(left_rows, right_rows):
    return lax.dot_general(
        left_rows, right_rows, (((0,), (0,)), ((), ())), preferred_element_type=F32
    )


def back_dot(gradient, weight):
    return lax.dot_general(
        gradient, weight, (((1,), (1,)), ((), ())), preferred_element_type=F32
    )


def softmax_block(query, key, same):
    scores = jnp.where(same, back_dot(query, key) * SCALE, -1e30)
    exponent = jnp.exp(scores - jnp.max(scores, axis=-1, keepdims=True))
    return exponent / jnp.sum(exponent, axis=-1, keepdims=True)


def head_masks(rows):
    lane = lax.broadcasted_iota(jnp.int32, (rows, LANES), 1)
    return [lane < HEAD_DIM, lane >= HEAD_DIM]


def forward_kernel(qid_ref, kid_ref, q_ref, k_ref, v_ref, out_ref):
    rows = q_ref.shape[0]
    masks = head_masks(QB)
    for start in range(0, rows, QB):
        here = pl.ds(start, QB)
        window = pl.ds(start, QB + 2 * PAD)
        same = qid_ref[here, :] == kid_ref[:, window]
        query, key, value = q_ref[here, :], k_ref[window, :], v_ref[window, :]
        results = []
        for mask in masks:
            part = jnp.where(mask, query, jnp.zeros_like(query))
            attention = softmax_block(part, key, same).astype(BF16)
            results.append(jnp.dot(attention, value, preferred_element_type=F32))
        out_ref[here, :] = jnp.where(masks[0], results[0], results[1]).astype(BF16)


def backward_kernel(
    qid_ref, kid_ref, q_ref, k_ref, v_ref, da_ref, dq_ref, dk_ref, dv_ref
):
    rows = q_ref.shape[0]
    masks = head_masks(QB)
    dk_ref[...] = jnp.zeros_like(dk_ref)
    dv_ref[...] = jnp.zeros_like(dv_ref)
    wide = head_masks(QB + 2 * PAD)[0]
    for start in range(0, rows, QB):
        here = pl.ds(start, QB)
        window = pl.ds(start, QB + 2 * PAD)
        same = qid_ref[here, :] == kid_ref[:, window]
        query, key, value = q_ref[here, :], k_ref[window, :], v_ref[window, :]
        grads = da_ref[here, :]
        dqs, dks, dvs = [], [], []
        for mask in masks:
            part = jnp.where(mask, query, jnp.zeros_like(query))
            attention = softmax_block(part, key, same)
            grad_attention = back_dot(jnp.where(mask, grads, jnp.zeros_like(grads)), value)
            inner = jnp.sum(attention * grad_attention, axis=-1, keepdims=True)
            grad_scores = (attention * (grad_attention - inner)).astype(BF16)
            dqs.append(jnp.dot(grad_scores, key, preferred_element_type=F32))
            dks.append(outer_sum(grad_scores, query))
            dvs.append(outer_sum(attention.astype(BF16), grads))
        dq_ref[here, :] = (jnp.where(masks[0], dqs[0], dqs[1]) * SCALE).astype(BF16)
        dk_ref[window, :] += jnp.where(wide, dks[0], dks[1]) * SCALE
        dv_ref[window, :] += jnp.where(wide, dvs[0], dvs[1])


def attention_specs(rows, ext_rows, width):
    pairs = width // LANES
    return [
        pl.BlockSpec((rows, 1), lambda h: (0, 0)),
        pl.BlockSpec((1, ext_rows), lambda h: (0, 0)),
        pl.BlockSpec((rows, LANES), lambda h: (0, h)),
        pl.BlockSpec((ext_rows, LANES), lambda h: (0, h)),
        pl.BlockSpec((ext_rows, LANES), lambda h: (0, pairs + h)),
    ]


def attend_forward(qids, kids, projected, kv_ext, width):
    rows, ext_rows = projected.shape[0], kv_ext.shape[0]
    work = HEADS * rows * (QB + 2 * PAD)
    return pl.pallas_call(
        forward_kernel,
        grid=(width // LANES,),
        in_specs=attention_specs(rows, ext_rows, width),
        out_specs=pl.BlockSpec((rows, LANES), lambda h: (0, h)),
        out_shape=jax.ShapeDtypeStruct((rows, width), BF16),
        compiler_params=pltpu.CompilerParams(vmem_limit_bytes=40 * 1024 * 1024),
        cost_estimate=pl.CostEstimate(
            flops=8 * work * LANES, bytes_accessed=6 * 1024 * 1024, transcendentals=work
        ),
    )(qids, kids, projected, kv_ext, kv_ext)


def attend_backward(qids, kids, projected, kv_ext, grad_mixed, width):
    rows, ext_rows = projected.shape[0], kv_ext.shape[0]
    work = HEADS * rows * (QB + 2 * PAD)
    return pl.pallas_call(
        backward_kernel,
        grid=(width // LANES,),
        in_specs=attention_specs(rows, ext_rows, width)
        + [pl.BlockSpec((rows, LANES), lambda h: (0, h))],
        out_specs=[
            pl.BlockSpec((rows, LANES), lambda h: (0, h)),
            pl.BlockSpec((ext_rows, LANES), lambda h: (0, h)),
            pl.BlockSpec((ext_rows, LANES), lambda h: (0, h)),
        ],
        out_shape=[
            jax.ShapeDtypeStruct((rows, width), BF16),
            jax.ShapeDtypeStruct((ext_rows, width), F32),
            jax.ShapeDtypeStruct((ext_rows, width), F32),
        ],
        compiler_params=pltpu.CompilerParams(vmem_limit_bytes=40 * 1024 * 1024),
        cost_estimate=pl.CostEstimate(
            flops=16 * work * LANES, bytes_accessed=16 * 1024 * 1024, transcendentals=work
        ),
    )(qids, kids, projected, kv_ext, kv_ext, grad_mixed)


def per_device(
    tokens, cotangent, image_ids, w_qkv, w_out, w_up, w_down, gains, shifts, biases, bias_up
):
    rows, width = tokens.shape
    count = lax.axis_size("fsdp")
    device = lax.axis_index("fsdp")
    orders = bit_orders(count)
    order_qkv, order_up, order_down = orders(0), orders(1), orders(2)
    own_cols = gains.shape[2]
    own_up = bias_up.shape[1]
    up_chain = [(i, i + 1) for i in range(count - 1)]
    down_chain = [(i + 1, i) for i in range(count - 1)]

    padded_ids = jnp.concatenate(
        [jnp.full((PAD,), -1, jnp.int32), image_ids, jnp.full((PAD,), -2, jnp.int32)]
    )
    ext_ids = lax.dynamic_slice_in_dim(padded_ids, device * rows, rows + 2 * PAD, 0)
    kids = ext_ids[None, :]
    qids = ext_ids[PAD : PAD + rows][:, None]

    small = jnp.concatenate(
        [gains[0].reshape(-1), shifts[0].reshape(-1), biases[0].reshape(-1), bias_up[0]]
    )
    small_len = small.shape[0]
    small_pad = -(-small_len // 1024) * 1024
    small = jnp.pad(small, (0, small_pad - small_len)).reshape(-1, LANES)
    small_full = gather_rows(small, order_qkv).reshape(count, small_pad).astype(F32)
    vectors = small_full[:, : 8 * own_cols].reshape(count, 8, own_cols)
    vectors = jnp.transpose(vectors, (1, 0, 2)).reshape(8, width)
    gain_f, shift_f, bias_f = vectors[0:2], vectors[2:4], vectors[4:8]
    up_bias_f = small_full[:, 8 * own_cols : small_len].reshape(count * own_up)

    qkv_full = gather_rows(w_qkv[0], order_qkv).reshape(width, 3 * width)
    out_full = gather_rows(w_out[0], order_up).reshape(width, width)
    up_full = gather_rows(w_up[0], order_up).reshape(width, -1)
    down_full = gather_rows(w_down[0], order_down).reshape(-1, width)

    source = tokens.astype(F32)
    target = cotangent.astype(F32)
    n1, r1 = centered(source)
    h1 = (n1 * gain_f[0] + shift_f[0]).astype(BF16)
    qkv_bias = jnp.concatenate([bias_f[0], jnp.zeros_like(bias_f[0]), bias_f[1]])
    projected = (jnp.dot(h1, qkv_full, preferred_element_type=F32) + qkv_bias).astype(BF16)
    kv = projected[:, width:]
    gap = jnp.zeros((PAD - RIM, 2 * width), BF16)
    kv_ext = jnp.concatenate(
        [
            gap,
            lax.ppermute(kv[rows - RIM :], "fsdp", up_chain),
            kv,
            lax.ppermute(kv[:RIM], "fsdp", down_chain),
            gap,
        ],
        axis=0,
    )
    mixed = attend_forward(qids, kids, projected, kv_ext, width)
    middle = source + (jnp.dot(mixed, out_full, preferred_element_type=F32) + bias_f[2])
    n2, r2 = centered(middle)
    h2 = (n2 * gain_f[1] + shift_f[1]).astype(BF16)
    before = jnp.dot(h2, up_full, preferred_element_type=F32) + up_bias_f
    cdf = 0.5 * (1.0 + lax.erf(before * (0.5**0.5)))
    slope = cdf + before * jnp.exp(-0.5 * before * before) * ((2.0 * math.pi) ** -0.5)
    activated = (before * cdf).astype(BF16)
    activated, slope = lax.optimization_barrier((activated, slope))
    result = middle + (jnp.dot(activated, down_full, preferred_element_type=F32) + bias_f[3])

    low_cot = cotangent
    grad_down = scatter_sum(
        outer_sum(activated, low_cot).reshape(count, -1, width), order_down, BF16
    )
    sum_down = jnp.sum(target, axis=0)
    grad_before = (back_dot(low_cot, down_full) * slope).astype(BF16)
    grad_up = scatter_sum(
        outer_sum(h2, grad_before).reshape(count, own_cols, -1), order_up, BF16
    )
    sum_up = jnp.sum(grad_before.astype(F32), axis=0)
    grad_h2 = back_dot(grad_before, up_full)
    gain_two = jnp.sum(grad_h2 * n2, axis=0)
    shift_two = jnp.sum(grad_h2, axis=0)
    grad_middle = target + norm_back(grad_h2, n2, r2, gain_f[1])
    branch = grad_middle.astype(BF16)
    grad_out = scatter_sum(
        outer_sum(mixed, branch).reshape(count, own_cols, -1), order_up, BF16
    )
    sum_out = jnp.sum(branch.astype(F32), axis=0)
    grad_mixed = back_dot(branch, out_full).astype(BF16)
    dq, dk, dv = attend_backward(qids, kids, projected, kv_ext, grad_mixed, width)
    low_rim = jnp.concatenate([dk[PAD - RIM : PAD], dv[PAD - RIM : PAD]], axis=1).astype(BF16)
    high_start = PAD + rows
    high_rim = jnp.concatenate(
        [dk[high_start : high_start + RIM], dv[high_start : high_start + RIM]], axis=1
    ).astype(BF16)
    from_above = lax.ppermute(low_rim, "fsdp", down_chain).astype(F32)
    from_below = lax.ppermute(high_rim, "fsdp", up_chain).astype(F32)
    own = jnp.concatenate([dk[PAD:high_start], dv[PAD:high_start]], axis=1)
    own = own + jnp.pad(from_below, ((0, rows - RIM), (0, 0)))
    own = own + jnp.pad(from_above, ((rows - RIM, 0), (0, 0)))
    grad_proj = jnp.concatenate([dq, own.astype(BF16)], axis=1)
    grad_qkv = scatter_sum(
        outer_sum(h1, grad_proj).reshape(count, own_cols, -1), order_qkv, BF16
    )
    sums = jnp.sum(grad_proj.astype(F32), axis=0)
    grad_h1 = back_dot(grad_proj, qkv_full)
    gain_one = jnp.sum(grad_h1 * n1, axis=0)
    shift_one = jnp.sum(grad_h1, axis=0)
    grad_tokens = grad_middle + norm_back(grad_h1, n1, r1, gain_f[0])

    stacked = jnp.stack(
        [
            gain_one,
            gain_two,
            shift_one,
            shift_two,
            sums[:width],
            sums[2 * width :],
            sum_out,
            sum_down,
        ],
        axis=0,
    )
    stacked = jnp.transpose(stacked.reshape(8, count, own_cols), (1, 0, 2))
    packed = jnp.concatenate(
        [stacked.reshape(count, 8 * own_cols), sum_up.reshape(count, own_up)], axis=1
    )
    packed = jnp.pad(packed, ((0, 0), (0, small_pad - small_len)))
    packed = scatter_sum(packed.reshape(count, -1, LANES), order_qkv, F32).reshape(-1)
    vector_grads = packed[: 8 * own_cols].reshape(8, own_cols)
    return (
        result.astype(BF16),
        grad_tokens,
        grad_qkv[None],
        grad_out[None],
        grad_up[None],
        grad_down[None],
        vector_grads[None, 0:2],
        vector_grads[None, 2:4],
        vector_grads[None, 4:8],
        packed[8 * own_cols : small_len][None],
    )


def solution(mesh):
    in_specs = (
        P("fsdp", None),
        P("fsdp", None),
        P(),
        P(None, "fsdp", None),
        P(None, "fsdp", None),
        P(None, "fsdp", None),
        P(None, "fsdp", None),
        P(None, None, "fsdp"),
        P(None, None, "fsdp"),
        P(None, None, "fsdp"),
        P(None, "fsdp"),
    )
    out_specs = (
        P("fsdp", None),
        P("fsdp", None),
        P(None, "fsdp", None),
        P(None, "fsdp", None),
        P(None, "fsdp", None),
        P(None, "fsdp", None),
        P(None, None, "fsdp"),
        P(None, None, "fsdp"),
        P(None, None, "fsdp"),
        P(None, "fsdp"),
    )
    return jax.shard_map(
        per_device, mesh=mesh, in_specs=in_specs, out_specs=out_specs, check_vma=False
    )
```

```python
import math

import jax
import jax.numpy as jnp
from jax import lax
from jax.experimental import pallas as pl
from jax.experimental.pallas import tpu as pltpu
from jax.sharding import PartitionSpec as P

HEADS = 12
HEAD_DIM = 64
RIM = 208
PAD = 256
QB = 256
LANES = 128
SCALE = HEAD_DIM ** (-0.5)
F32 = jnp.float32
BF16 = jnp.bfloat16


def bit_orders(count):
    bits = int(math.log2(count))
    rest = list(range(1, bits))

    def rotated(by):
        return [0] + rest[by:] + rest[:by]

    return rotated


def partner_pairs(count, bit):
    return [(i, i ^ (1 << bit)) for i in range(count)]


def gather_rows(shard, order):
    count = lax.axis_size("fsdp")
    me = lax.axis_index("fsdp")
    have = []
    block = shard[None]
    for bit in reversed(order):
        other = lax.ppermute(block, "fsdp", partner_pairs(count, bit))
        mine_high = ((me >> bit) & 1) == 1
        low = jnp.where(mine_high, other, block)
        high = jnp.where(mine_high, block, other)
        higher = sum(1 for b in have if b > bit)
        lower = len(have) - higher
        lead = (1 << higher, 1 << lower)
        low = low.reshape(lead + shard.shape)
        high = high.reshape(lead + shard.shape)
        block = jnp.stack([low, high], axis=1).reshape((-1,) + shard.shape)
        have.append(bit)
    return block


def scatter_sum(parts, order, send_type):
    return scatter_steps(parts, order, order, send_type)[0]


def scatter_steps(parts, order, unsplit, send_type):
    count = lax.axis_size("fsdp")
    me = lax.axis_index("fsdp")
    shape = parts.shape[1:]
    left = set(unsplit)
    block = parts
    for bit in order:
        higher = sum(1 for b in left if b > bit)
        lower = len(left) - 1 - higher
        view = block.reshape((1 << higher, 2, 1 << lower) + shape)
        mine = (me >> bit) & 1
        keep = lax.dynamic_index_in_dim(view, mine, axis=1, keepdims=False)
        give = lax.dynamic_index_in_dim(view, 1 - mine, axis=1, keepdims=False).astype(send_type)
        give = give.reshape((-1,) + shape)
        got = lax.ppermute(give, "fsdp", partner_pairs(count, bit))
        block = keep.reshape((-1,) + shape).astype(F32) + got.astype(F32)
        left.remove(bit)
    return block


def centered(values):
    center = values - jnp.mean(values, axis=-1, keepdims=True)
    scale = lax.rsqrt(jnp.mean(center * center, axis=-1, keepdims=True) + 1e-06)
    return center * scale, scale


def norm_back(grad, normal, scale, gain):
    weighted = grad * gain
    mean_one = jnp.mean(weighted, axis=-1, keepdims=True)
    mean_two = jnp.mean(weighted * normal, axis=-1, keepdims=True)
    return scale * (weighted - mean_one - normal * mean_two)


def outer_sum(left_rows, right_rows):
    return lax.dot_general(
        left_rows, right_rows, (((0,), (0,)), ((), ())), preferred_element_type=F32
    )


def back_dot(gradient, weight):
    return lax.dot_general(
        gradient, weight, (((1,), (1,)), ((), ())), preferred_element_type=F32
    )


def softmax_block(query, key, same):
    scores = jnp.where(same, back_dot(query, key) * SCALE, -1e30)
    exponent = jnp.exp(scores - jnp.max(scores, axis=-1, keepdims=True))
    return exponent / jnp.sum(exponent, axis=-1, keepdims=True)


def head_masks(rows):
    lane = lax.broadcasted_iota(jnp.int32, (rows, LANES), 1)
    return [lane < HEAD_DIM, lane >= HEAD_DIM]


def forward_kernel(qid_ref, kid_ref, q_ref, k_ref, v_ref, out_ref):
    rows = q_ref.shape[0]
    masks = head_masks(QB)
    for start in range(0, rows, QB):
        here = pl.ds(start, QB)
        window = pl.ds(start, QB + 2 * PAD)
        same = qid_ref[here, :] == kid_ref[:, window]
        query, key, value = q_ref[here, :], k_ref[window, :], v_ref[window, :]
        results = []
        for mask in masks:
            part = jnp.where(mask, query, jnp.zeros_like(query))
            attention = softmax_block(part, key, same).astype(BF16)
            results.append(jnp.dot(attention, value, preferred_element_type=F32))
        out_ref[here, :] = jnp.where(masks[0], results[0], results[1]).astype(BF16)


def backward_kernel(
    qid_ref, kid_ref, q_ref, k_ref, v_ref, da_ref, dq_ref, dk_ref, dv_ref
):
    rows = q_ref.shape[0]
    masks = head_masks(QB)
    dk_ref[...] = jnp.zeros_like(dk_ref)
    dv_ref[...] = jnp.zeros_like(dv_ref)
    wide = head_masks(QB + 2 * PAD)[0]
    for start in range(0, rows, QB):
        here = pl.ds(start, QB)
        window = pl.ds(start, QB + 2 * PAD)
        same = qid_ref[here, :] == kid_ref[:, window]
        query, key, value = q_ref[here, :], k_ref[window, :], v_ref[window, :]
        grads = da_ref[here, :]
        dqs, dks, dvs = [], [], []
        for mask in masks:
            part = jnp.where(mask, query, jnp.zeros_like(query))
            attention = softmax_block(part, key, same)
            grad_attention = back_dot(jnp.where(mask, grads, jnp.zeros_like(grads)), value)
            inner = jnp.sum(attention * grad_attention, axis=-1, keepdims=True)
            grad_scores = (attention * (grad_attention - inner)).astype(BF16)
            dqs.append(jnp.dot(grad_scores, key, preferred_element_type=F32))
            dks.append(outer_sum(grad_scores, query))
            dvs.append(outer_sum(attention.astype(BF16), grads))
        dq_ref[here, :] = (jnp.where(masks[0], dqs[0], dqs[1]) * SCALE).astype(BF16)
        dk_ref[window, :] += jnp.where(wide, dks[0], dks[1]) * SCALE
        dv_ref[window, :] += jnp.where(wide, dvs[0], dvs[1])


def attention_specs(rows, ext_rows, width):
    pairs = width // LANES
    return [
        pl.BlockSpec((rows, 1), lambda h: (0, 0)),
        pl.BlockSpec((1, ext_rows), lambda h: (0, 0)),
        pl.BlockSpec((rows, LANES), lambda h: (0, h)),
        pl.BlockSpec((ext_rows, LANES), lambda h: (0, h)),
        pl.BlockSpec((ext_rows, LANES), lambda h: (0, pairs + h)),
    ]


def attend_forward(qids, kids, projected, kv_ext, width):
    rows, ext_rows = projected.shape[0], kv_ext.shape[0]
    work = HEADS * rows * (QB + 2 * PAD)
    return pl.pallas_call(
        forward_kernel,
        grid=(width // LANES,),
        in_specs=attention_specs(rows, ext_rows, width),
        out_specs=pl.BlockSpec((rows, LANES), lambda h: (0, h)),
        out_shape=jax.ShapeDtypeStruct((rows, width), BF16),
        compiler_params=pltpu.CompilerParams(vmem_limit_bytes=40 * 1024 * 1024),
        cost_estimate=pl.CostEstimate(
            flops=8 * work * LANES, bytes_accessed=6 * 1024 * 1024, transcendentals=work
        ),
    )(qids, kids, projected, kv_ext, kv_ext)


def attend_backward(qids, kids, projected, kv_ext, grad_mixed, width):
    rows, ext_rows = projected.shape[0], kv_ext.shape[0]
    work = HEADS * rows * (QB + 2 * PAD)
    return pl.pallas_call(
        backward_kernel,
        grid=(width // LANES,),
        in_specs=attention_specs(rows, ext_rows, width)
        + [pl.BlockSpec((rows, LANES), lambda h: (0, h))],
        out_specs=[
            pl.BlockSpec((rows, LANES), lambda h: (0, h)),
            pl.BlockSpec((ext_rows, LANES), lambda h: (0, h)),
            pl.BlockSpec((ext_rows, LANES), lambda h: (0, h)),
        ],
        out_shape=[
            jax.ShapeDtypeStruct((rows, width), BF16),
            jax.ShapeDtypeStruct((ext_rows, width), F32),
            jax.ShapeDtypeStruct((ext_rows, width), F32),
        ],
        compiler_params=pltpu.CompilerParams(vmem_limit_bytes=40 * 1024 * 1024),
        cost_estimate=pl.CostEstimate(
            flops=16 * work * LANES, bytes_accessed=16 * 1024 * 1024, transcendentals=work
        ),
    )(qids, kids, projected, kv_ext, kv_ext, grad_mixed)


def per_device(
    tokens, cotangent, image_ids, w_qkv, w_out, w_up, w_down, gains, shifts, biases, bias_up
):
    rows, width = tokens.shape
    count = lax.axis_size("fsdp")
    device = lax.axis_index("fsdp")
    orders = bit_orders(count)
    order_qkv, order_up, order_down = orders(0), orders(1), orders(2)
    own_cols = gains.shape[2]
    own_up = bias_up.shape[1]
    up_chain = [(i, i + 1) for i in range(count - 1)]
    down_chain = [(i + 1, i) for i in range(count - 1)]

    padded_ids = jnp.concatenate(
        [jnp.full((PAD,), -1, jnp.int32), image_ids, jnp.full((PAD,), -2, jnp.int32)]
    )
    ext_ids = lax.dynamic_slice_in_dim(padded_ids, device * rows, rows + 2 * PAD, 0)
    kids = ext_ids[None, :]
    qids = ext_ids[PAD : PAD + rows][:, None]

    small = jnp.concatenate(
        [gains[0].reshape(-1), shifts[0].reshape(-1), biases[0].reshape(-1), bias_up[0]]
    )
    small_len = small.shape[0]
    small_pad = -(-small_len // 1024) * 1024
    small = jnp.pad(small, (0, small_pad - small_len)).reshape(-1, LANES)
    small_full = gather_rows(small, order_qkv).reshape(count, small_pad).astype(F32)
    vectors = small_full[:, : 8 * own_cols].reshape(count, 8, own_cols)
    vectors = jnp.transpose(vectors, (1, 0, 2)).reshape(8, width)
    gain_f, shift_f, bias_f = vectors[0:2], vectors[2:4], vectors[4:8]
    up_bias_f = small_full[:, 8 * own_cols : small_len].reshape(count * own_up)

    qkv_full = gather_rows(w_qkv[0], order_qkv).reshape(width, 3 * width)
    out_full = gather_rows(w_out[0], order_up).reshape(width, width)
    up_full = gather_rows(w_up[0], order_up).reshape(width, -1)
    down_full = gather_rows(w_down[0], order_down).reshape(-1, width)

    source = tokens.astype(F32)
    target = cotangent.astype(F32)
    n1, r1 = centered(source)
    h1 = (n1 * gain_f[0] + shift_f[0]).astype(BF16)
    qkv_bias = jnp.concatenate([bias_f[0], jnp.zeros_like(bias_f[0]), bias_f[1]])
    projected = (jnp.dot(h1, qkv_full, preferred_element_type=F32) + qkv_bias).astype(BF16)
    kv = projected[:, width:]
    gap = jnp.zeros((PAD - RIM, 2 * width), BF16)
    kv_ext = jnp.concatenate(
        [
            gap,
            lax.ppermute(kv[rows - RIM :], "fsdp", up_chain),
            kv,
            lax.ppermute(kv[:RIM], "fsdp", down_chain),
            gap,
        ],
        axis=0,
    )
    mixed = attend_forward(qids, kids, projected, kv_ext, width)
    middle = source + (jnp.dot(mixed, out_full, preferred_element_type=F32) + bias_f[2])
    n2, r2 = centered(middle)
    h2 = (n2 * gain_f[1] + shift_f[1]).astype(BF16)
    before = jnp.dot(h2, up_full, preferred_element_type=F32) + up_bias_f
    cdf = 0.5 * (1.0 + lax.erf(before * (0.5**0.5)))
    slope = cdf + before * jnp.exp(-0.5 * before * before) * ((2.0 * math.pi) ** -0.5)
    activated = (before * cdf).astype(BF16)
    activated, slope = lax.optimization_barrier((activated, slope))
    result = middle + (jnp.dot(activated, down_full, preferred_element_type=F32) + bias_f[3])

    low_cot = cotangent
    half_down = scatter_steps(
        outer_sum(activated, low_cot).reshape(count, -1, width), order_down[:1], order_down, BF16
    )
    sum_down = jnp.sum(target, axis=0)
    grad_before = (back_dot(low_cot, down_full) * slope).astype(BF16)
    half_up = scatter_steps(
        outer_sum(h2, grad_before).reshape(count, own_cols, -1), order_up[:1], order_up, BF16
    )
    sum_up = jnp.sum(grad_before.astype(F32), axis=0)
    grad_h2 = back_dot(grad_before, up_full)
    gain_two = jnp.sum(grad_h2 * n2, axis=0)
    shift_two = jnp.sum(grad_h2, axis=0)
    grad_middle = target + norm_back(grad_h2, n2, r2, gain_f[1])
    branch = grad_middle.astype(BF16)
    grad_out = scatter_sum(
        outer_sum(mixed, branch).reshape(count, own_cols, -1), order_up, BF16
    )
    sum_out = jnp.sum(branch.astype(F32), axis=0)
    grad_mixed = back_dot(branch, out_full).astype(BF16)
    grad_mixed, half_down, half_up = lax.optimization_barrier((grad_mixed, half_down, half_up))
    grad_down = scatter_steps(half_down, order_down[1:], order_down[1:], BF16)[0]
    grad_up = scatter_steps(half_up, order_up[1:], order_up[1:], BF16)[0]
    dq, dk, dv = attend_backward(qids, kids, projected, kv_ext, grad_mixed, width)
    low_rim = jnp.concatenate([dk[PAD - RIM : PAD], dv[PAD - RIM : PAD]], axis=1).astype(BF16)
    high_start = PAD + rows
    high_rim = jnp.concatenate(
        [dk[high_start : high_start + RIM], dv[high_start : high_start + RIM]], axis=1
    ).astype(BF16)
    from_above = lax.ppermute(low_rim, "fsdp", down_chain).astype(F32)
    from_below = lax.ppermute(high_rim, "fsdp", up_chain).astype(F32)
    own = jnp.concatenate([dk[PAD:high_start], dv[PAD:high_start]], axis=1)
    own = own + jnp.pad(from_below, ((0, rows - RIM), (0, 0)))
    own = own + jnp.pad(from_above, ((rows - RIM, 0), (0, 0)))
    grad_proj = jnp.concatenate([dq, own.astype(BF16)], axis=1)
    grad_qkv = scatter_sum(
        outer_sum(h1, grad_proj).reshape(count, own_cols, -1), order_qkv, BF16
    )
    sums = jnp.sum(grad_proj.astype(F32), axis=0)
    grad_h1 = back_dot(grad_proj, qkv_full)
    gain_one = jnp.sum(grad_h1 * n1, axis=0)
    shift_one = jnp.sum(grad_h1, axis=0)
    grad_tokens = grad_middle + norm_back(grad_h1, n1, r1, gain_f[0])

    stacked = jnp.stack(
        [
            gain_one,
            gain_two,
            shift_one,
            shift_two,
            sums[:width],
            sums[2 * width :],
            sum_out,
            sum_down,
        ],
        axis=0,
    )
    stacked = jnp.transpose(stacked.reshape(8, count, own_cols), (1, 0, 2))
    packed = jnp.concatenate(
        [stacked.reshape(count, 8 * own_cols), sum_up.reshape(count, own_up)], axis=1
    )
    packed = jnp.pad(packed, ((0, 0), (0, small_pad - small_len)))
    packed = scatter_sum(packed.reshape(count, -1, LANES), order_qkv, F32).reshape(-1)
    vector_grads = packed[: 8 * own_cols].reshape(8, own_cols)
    return (
        result.astype(BF16),
        grad_tokens,
        grad_qkv[None],
        grad_out[None],
        grad_up[None],
        grad_down[None],
        vector_grads[None, 0:2],
        vector_grads[None, 2:4],
        vector_grads[None, 4:8],
        packed[8 * own_cols : small_len][None],
    )


def solution(mesh):
    in_specs = (
        P("fsdp", None),
        P("fsdp", None),
        P(),
        P(None, "fsdp", None),
        P(None, "fsdp", None),
        P(None, "fsdp", None),
        P(None, "fsdp", None),
        P(None, None, "fsdp"),
        P(None, None, "fsdp"),
        P(None, None, "fsdp"),
        P(None, "fsdp"),
    )
    out_specs = (
        P("fsdp", None),
        P("fsdp", None),
        P(None, "fsdp", None),
        P(None, "fsdp", None),
        P(None, "fsdp", None),
        P(None, "fsdp", None),
        P(None, None, "fsdp"),
        P(None, None, "fsdp"),
        P(None, None, "fsdp"),
        P(None, "fsdp"),
    )
    return jax.shard_map(
        per_device, mesh=mesh, in_specs=in_specs, out_specs=out_specs, check_vma=False
    )
```
